32 devices in a mesh: row: 8 (over y, x, core), col: 4 (over z).
Axes of the slice: x: 2, y: 2, z: 4, core: 2. Of those that a mesh axis runs over, the one named last changes fastest.
Arguments:
- tokens: bfloat16 [512, 12288], P('row', 'col'), may hold values from -6 to 6
- out_grad: bfloat16 [512, 12288], P('row', 'col'), may hold values from -6 to 6
- w_in: bfloat16 [12288, 24576], P('col', 'row'), may hold values from -0.0546875 to 0.0546875
- w_out: bfloat16 [24576, 12288], P('row', 'col'), may hold values from -0.0390625 to 0.0390625
- bias_in: float32 [24576], P('row'), may hold values from -3 to 3
- stream_ids: int32 [3], replicated, may hold values from 0 to 4095
- tile_keys: int32 [64, 192], replicated, may hold values from 0 to 16777215
Outputs:
- grad_tokens: bfloat16 [512, 12288], P('row', 'col')
- grad_w_in: bfloat16 [12288, 24576], P('col', 'row')
- grad_w_out: bfloat16 [24576, 12288], P('row', 'col')
- grad_bias_in: float32 [24576], P('row')
- grad_bias_out: float32 [12288], P('col')
The draws below stay inside these ranges and needn't reach their ends.
All inputs are finite; a program needn't handle non-finite values.
Results may differ from the reference program's by a relative error of at most 0.005.
Values may be sent and summed in bfloat16 or wider, within the bound.
A program may use at most 192 MiB of HBM per device.

```python
import jax
import jax.numpy as jnp
from jax import lax

D = 12288
FF = 24576
TOKENS = 512
TILE_T = 8
TILE_F = 128


def with_ends(result, stream_key, low, high):
    longest = result.shape.index(max(result.shape))
    spots = []
    for shift in (0, 1):
        where = [jax.random.randint(jax.random.fold_in(stream_key, axis), (), 0, length) for axis, length in enumerate(result.shape)]
        where[longest] = (where[longest] + shift) % result.shape[longest]
        spots.append(tuple(where))
    return result.at[spots[0]].set(low).at[spots[1]].set(high)


def levels(own_key, extent, pieces, least, high):
    level = 1.0
    for position, parts in pieces:
        heights = jax.random.uniform(jax.random.fold_in(jax.random.fold_in(own_key, 6), position), (parts,), jnp.float32, least / len(pieces), high / len(pieces))
        level = level * jnp.repeat(jnp.exp(heights), extent[position] // parts).reshape((-1,) + (1,) * (len(extent) - 1 - position))
    return level


def gaussian(rng, shape, scale, limit, shards=(), kind=jnp.bfloat16):
    result = jax.random.normal(rng, shape, jnp.float32) * scale
    if len(shards) > 0:
        result = levels(rng, shape, shards, -0.22, 0.18) * result
    return jnp.clip(result, min=-limit, max=limit).astype(kind)


def setup_inputs(seed: int = 0) -> dict:
    splits = jax.random.split(jax.random.key(seed), 8)
    tokens = gaussian(splits[0], (TOKENS, D), 1.0, 6.0, ((0, 8), (1, 4)))
    out_grad = gaussian(splits[1], (TOKENS, D), 1.0, 6.0, ((0, 8), (1, 4)))
    w_in = gaussian(splits[2], (D, FF), D ** -0.5, 0.0546875, ((0, 4), (1, 8)))
    w_out = gaussian(splits[3], (FF, D), FF ** -0.5, 0.0390625, ((0, 8), (1, 4)))
    bias_in = gaussian(splits[4], (FF,), 0.5, 3.0, ((0, 8),), jnp.float32)
    stream_ids = jax.random.randint(splits[5], (3,), 0, 4096).astype(jnp.int32)
    tile_keys = with_ends(jax.random.randint(splits[6], (TOKENS // TILE_T, FF // TILE_F), 0, 16777216), jax.random.fold_in(splits[6], 1), 0, 16777215).astype(jnp.int32)
    return {"tokens": tokens, "out_grad": out_grad, "w_in": w_in, "w_out": w_out, "bias_in": bias_in, "stream_ids": stream_ids, "tile_keys": tile_keys}


mix_one = 73856093
mix_two = 19349663
mix_three = 83492791
golden = -1640531535
mult_one = 2146121005
mult_two = -2073254261


def shift_down(value, count):
    return lax.shift_right_logical(value, jnp.full(value.shape, count, jnp.int32))


def keep_mask(tile_keys, stream_ids, row_start, row_count, col_start, col_count, tile_t, tile_f):
    row_ids = row_start + jnp.arange(row_count, dtype=jnp.int32)
    col_ids = col_start + jnp.arange(col_count, dtype=jnp.int32)
    onehot_rows = (row_ids[:, None] // tile_t == jnp.arange(tile_keys.shape[0], dtype=jnp.int32)[None, :]).astype(jnp.int32)
    onehot_cols = (jnp.arange(tile_keys.shape[1], dtype=jnp.int32)[:, None] == col_ids[None, :] // tile_f).astype(jnp.int32)
    picked = jnp.dot(onehot_rows, tile_keys, preferred_element_type=jnp.int32)
    picked = jnp.dot(picked, onehot_cols, preferred_element_type=jnp.int32)
    salt = (stream_ids[0] * jnp.int32(mix_one)) ^ (stream_ids[1] * jnp.int32(mix_two)) ^ (stream_ids[2] * jnp.int32(mix_three))
    offset = (row_ids[:, None] % tile_t) * tile_f + col_ids[None, :] % tile_f
    value = (picked ^ salt) + offset * jnp.int32(golden)
    value = value ^ shift_down(value, 16)
    value = value * jnp.int32(mult_one)
    value = value ^ shift_down(value, 15)
    value = value * jnp.int32(mult_two)
    value = value ^ shift_down(value, 16)
    return ((shift_down(value, 8) & jnp.int32(1023)) < jnp.int32(922)).astype(jnp.float32)


def normal_cdf(value):
    return 0.5 * (1.0 + lax.erf(value * 0.7071067811865476))


def reference(tokens, out_grad, w_in, w_out, bias_in, stream_ids, tile_keys):
    pre = jnp.dot(tokens, w_in, preferred_element_type=jnp.float32) + bias_in.astype(jnp.float32)
    keep = keep_mask(tile_keys, stream_ids, 0, TOKENS, 0, FF, TILE_T, TILE_F)
    scaled = keep * (1.0 / 0.9)
    cdf = normal_cdf(pre)
    act = (pre * cdf * scaled).astype(jnp.bfloat16)
    dact = lax.dot_general(out_grad, w_out, (((1,), (1,)), ((), ())), preferred_element_type=jnp.float32)
    slope = cdf + pre * jnp.exp(-0.5 * pre * pre) * 0.3989422804014327
    dpre = (dact * scaled * slope).astype(jnp.bfloat16)
    grad_w_out = lax.dot_general(act, out_grad, (((0,), (0,)), ((), ())), preferred_element_type=jnp.float32).astype(jnp.bfloat16)
    grad_w_in = lax.dot_general(tokens, dpre, (((0,), (0,)), ((), ())), preferred_element_type=jnp.float32).astype(jnp.bfloat16)
    grad_tokens = lax.dot_general(dpre, w_in, (((1,), (1,)), ((), ())), preferred_element_type=jnp.float32).astype(jnp.bfloat16)
    grad_bias_in = jnp.sum(dpre.astype(jnp.float32), axis=0)
    grad_bias_out = jnp.sum(out_grad.astype(jnp.float32), axis=0)
    return (grad_tokens, grad_w_in, grad_w_out, grad_bias_in, grad_bias_out)
```

```python
import functools

import jax
import jax.numpy as jnp
from jax import lax
from jax.experimental import pallas as pl
from jax.experimental.pallas import tpu as pltpu
from jax.sharding import PartitionSpec as P

TILE_T = 8
TILE_F = 128
MESH = pl.DeviceIdType.MESH


mix_one = 73856093
mix_two = 19349663
mix_three = 83492791
golden = -1640531535
mult_one = 2146121005
mult_two = -2073254261


def shift_down(value, count):
    return lax.shift_right_logical(value, jnp.full(value.shape, count, jnp.int32))


def keep_mask(tile_keys, stream_ids, first_tile, tile_count, per_chunk):
    salt = (
        stream_ids[0] * jnp.int32(mix_one)
        ^ stream_ids[1] * jnp.int32(mix_two)
        ^ stream_ids[2] * jnp.int32(mix_three)
    )
    token_tiles = tile_keys.shape[0]
    chunks = tile_count // per_chunk
    keys = lax.dynamic_slice_in_dim(tile_keys, first_tile, tile_count, 1) ^ salt
    keys = keys.reshape(token_tiles, chunks, per_chunk).transpose(1, 0, 2)
    shape = (chunks, token_tiles, TILE_T, per_chunk, TILE_F)
    offset = lax.broadcasted_iota(jnp.int32, shape, 2) * TILE_F + lax.broadcasted_iota(
        jnp.int32, shape, 4
    )
    value = keys[:, :, None, :, None] + offset * jnp.int32(golden)
    value = value ^ shift_down(value, 16)
    value = value * jnp.int32(mult_one)
    value = value ^ shift_down(value, 15)
    value = value * jnp.int32(mult_two)
    value = value ^ shift_down(value, 16)
    keep = (shift_down(value, 8) & jnp.int32(1023)) < jnp.int32(922)
    return keep.astype(jnp.bfloat16).reshape(chunks, token_tiles * TILE_T, per_chunk * TILE_F)


def exchange_kernel(
    n, units, slots, rows,
    tokens, grads, w_in, w_out, bias, keep,
    act, dpre, acc, bias_sum,
    own, from_left, from_right, to_right, to_left, in_ring, out_ring,
    in_sem, out_sem, right_send, right_recv, left_send, left_recv,
):
    me = lax.axis_index("col")
    right, left = lax.rem(me + 1, n), lax.rem(me + n - 1, n)
    total_rows, width = own.shape[1], own.shape[2]
    model = in_ring.shape[1]
    chunks = units // 2
    far = jnp.maximum(me, n - 1 - me)

    def fetch_in(c):
        slot = lax.rem(c, slots)
        cols = pl.ds(pl.multiple_of(c * width, width), width)
        return pltpu.make_async_copy(w_in.at[:, cols], in_ring.at[slot], in_sem.at[slot])

    def fetch_out(c):
        slot = lax.rem(c, 2)
        cols = pl.ds(pl.multiple_of(c * width, width), width)
        return pltpu.make_async_copy(w_out.at[cols, :], out_ring.at[slot], out_sem.at[slot])

    def send_right(q):
        return pltpu.make_async_remote_copy(
            src_ref=to_right.at[lax.rem(q, 2)], dst_ref=from_left.at[q],
            send_sem=right_send.at[lax.rem(q, 2)], recv_sem=right_recv.at[q],
            device_id={"col": right}, device_id_type=MESH,
        )

    def send_left(q):
        return pltpu.make_async_remote_copy(
            src_ref=to_left.at[lax.rem(q, 2)], dst_ref=from_right.at[q],
            send_sem=left_send.at[lax.rem(q, 2)], recv_sem=left_recv.at[q],
            device_id={"col": left}, device_id_type=MESH,
        )

    def own_unit(q):
        c = q // 2

        @pl.when(lax.rem(q, 2) == 0)
        def _():
            fetch_in(c).wait()

            @pl.when(c + 1 < chunks)
            def _():
                fetch_in(c + 1).start()
                fetch_out(c + 1).start()

            own[q] = jnp.dot(
                tokens[...], in_ring[lax.rem(c, slots)], preferred_element_type=jnp.float32
            )

        @pl.when(lax.rem(q, 2) == 1)
        def _():
            fetch_out(c).wait()
            own[q] = lax.dot_general(
                grads[...], out_ring[lax.rem(c, 2)], (((1,), (1,)), ((), ())),
                preferred_element_type=jnp.float32,
            )

    def pass_on(arrived, outgoing, copy, q, first, last):
        @pl.when(jnp.logical_not(first))
        def _():
            copy(q).wait_recv()

        @pl.when(jnp.logical_not(last))
        def _():
            @pl.when(q >= 2)
            def _():
                copy(q - 2).wait_send()

            @pl.when(first)
            def _():
                outgoing[lax.rem(q, 2)] = own[q].astype(outgoing.dtype)

            @pl.when(jnp.logical_not(first))
            def _():
                outgoing[lax.rem(q, 2)] = (
                    arrived[q].astype(jnp.float32) + own[q]
                ).astype(outgoing.dtype)

            copy(q).start()

    def finish(c):
        cols = pl.ds(pl.multiple_of(c * width, width), width)
        shift = bias[c]

        def add_arrived(q):
            @pl.when(me > 0)
            def _():
                own[q] += from_left[q].astype(jnp.float32)

            @pl.when(me < n - 1)
            def _():
                own[q] += from_right[q].astype(jnp.float32)

        add_arrived(2 * c)
        add_arrived(2 * c + 1)

        def block(k, total):
            at = pl.ds(pl.multiple_of(k * rows, rows), rows)
            pre = own[2 * c, at, :] + shift
            scaled = keep[c, at, :].astype(jnp.float32) * (1.0 / 0.9)
            cdf = 0.5 * (1.0 + lax.erf(pre * 0.7071067811865476))
            act[at, cols] = (pre * cdf * scaled).astype(act.dtype)
            slope = cdf + pre * jnp.exp(-0.5 * pre * pre) * 0.3989422804014327
            part = (own[2 * c + 1, at, :] * scaled * slope).astype(dpre.dtype)
            dpre[at, cols] = part
            return total + jnp.sum(part.astype(jnp.float32), axis=0, keepdims=True)

        bias_sum[c] = lax.fori_loop(
            0, total_rows // rows, block, jnp.zeros((1, width), jnp.float32)
        )
        slot = lax.rem(c, slots)

        def into(j, carry):
            at = pl.ds(pl.multiple_of(j * width, width), width)
            acc[:, at] += lax.dot_general(
                dpre[:, cols], in_ring[slot, at, :], (((1,), (1,)), ((), ())),
                preferred_element_type=jnp.float32,
            )
            return carry

        lax.fori_loop(0, model // width, into, 0)

    fetch_in(0).start()
    fetch_out(0).start()
    barrier = pltpu.get_barrier_semaphore()

    for peer in (left, right):
        pl.semaphore_signal(barrier, inc=1, device_id={"col": peer}, device_id_type=MESH)
    acc[...] = jnp.zeros_like(acc)
    own_unit(0)

    pl.semaphore_wait(barrier, 2)

    def step(s, carry):
        right_unit = s - me
        left_unit = s - (n - 1 - me)
        done = s - far

        @pl.when((right_unit >= 0) & (right_unit < units))
        def _():
            pass_on(from_left, to_right, send_right, right_unit, me == 0, me == n - 1)

        @pl.when((left_unit >= 0) & (left_unit < units))
        def _():
            pass_on(from_right, to_left, send_left, left_unit, me == n - 1, me == 0)

        @pl.when(s + 1 < units)
        def _():
            own_unit(s + 1)

        @pl.when((done >= 0) & (done < units) & (lax.rem(done + 2 * n, 2) == 1))
        def _():
            finish(done // 2)

        return carry

    lax.fori_loop(0, units + n - 1, step, 0)

    for q in (units - 2, units - 1):
        @pl.when(me < n - 1)
        def _():
            send_right(q).wait_send()

        @pl.when(me > 0)
        def _():
            send_left(q).wait_send()


def exchange(all_tokens, all_grads, w_in, w_out, bias, keep, n):
    total_rows, model = all_tokens.shape
    ff_local = w_in.shape[1]
    chunks, _, width = keep.shape
    units = 2 * chunks
    slots = n // 2 + 3
    vmem = pl.BlockSpec(memory_space=pltpu.VMEM)
    anywhere = pl.BlockSpec(memory_space=pl.ANY)
    unit_buffer = pltpu.VMEM((units, total_rows, width), jnp.bfloat16)
    unit_sems = pltpu.SemaphoreType.DMA((units,))
    return pl.pallas_call(
        functools.partial(exchange_kernel, n, units, slots, 32),
        out_shape=(
            jax.ShapeDtypeStruct((total_rows, ff_local), jnp.bfloat16),
            jax.ShapeDtypeStruct((total_rows, ff_local), jnp.bfloat16),
            jax.ShapeDtypeStruct((total_rows, model), jnp.float32),
            jax.ShapeDtypeStruct((chunks, 1, width), jnp.float32),
        ),
        in_specs=[vmem, vmem, anywhere, anywhere, vmem, vmem],
        out_specs=(vmem, vmem, vmem, vmem),
        scratch_shapes=[
            pltpu.VMEM((units, total_rows, width), jnp.float32),
            unit_buffer,
            unit_buffer,
            pltpu.VMEM((2, total_rows, width), jnp.bfloat16),
            pltpu.VMEM((2, total_rows, width), jnp.bfloat16),
            pltpu.VMEM((slots, model, width), jnp.bfloat16),
            pltpu.VMEM((2, width, model), jnp.bfloat16),
            pltpu.SemaphoreType.DMA((slots,)),
            pltpu.SemaphoreType.DMA((2,)),
            pltpu.SemaphoreType.DMA((2,)),
            unit_sems,
            pltpu.SemaphoreType.DMA((2,)),
            unit_sems,
        ],
        compiler_params=pltpu.CompilerParams(
            collective_id=0, has_side_effects=True, vmem_limit_bytes=63 * 1024 * 1024
        ),
        cost_estimate=pl.CostEstimate(
            flops=6 * total_rows * model * ff_local,
            bytes_accessed=4 * model * ff_local,
            transcendentals=2 * total_rows * ff_local,
        ),
    )(all_tokens, all_grads, w_in, w_out, bias, keep)


def local(tokens, out_grad, w_in, w_out, bias_in, stream_ids, tile_keys):
    col_count = lax.axis_size("col")
    row_index = lax.axis_index("row")
    col_index = lax.axis_index("col")
    ff_local = w_in.shape[1]
    width = 256
    chunks = ff_local // width
    all_tokens, all_grads = (
        lax.all_gather(tokens, "row", axis=0, tiled=True),
        lax.all_gather(out_grad, "row", axis=0, tiled=True),
    )
    tile_count = ff_local // TILE_F
    keep = keep_mask(tile_keys, stream_ids, row_index * tile_count, tile_count, width // TILE_F)
    act, dpre, token_terms, bias_sum = exchange(
        all_tokens, all_grads, w_in, w_out, bias_in.reshape(chunks, 1, width), keep, col_count
    )
    grad_tokens = lax.psum_scatter(
        token_terms, "row", scatter_dimension=0, tiled=True
    ).astype(jnp.bfloat16)
    grad_w_out = lax.dot_general(
        act, all_grads, (((0,), (0,)), ((), ())), preferred_element_type=jnp.float32
    ).astype(jnp.bfloat16)
    grad_w_in = lax.dot_general(
        all_tokens, dpre, (((0,), (0,)), ((), ())), preferred_element_type=jnp.float32
    ).astype(jnp.bfloat16)
    share = ff_local // col_count
    grad_bias_in = lax.all_gather(
        lax.dynamic_slice_in_dim(bias_sum.reshape(ff_local), col_index * share, share, 0),
        "col", axis=0, tiled=True,
    )
    grad_bias_out = jnp.sum(all_grads.astype(jnp.float32), axis=0)
    return (grad_tokens, grad_w_in, grad_w_out, grad_bias_in, grad_bias_out)


def solution(mesh):
    return jax.shard_map(
        local,
        mesh=mesh,
        in_specs=(
            P("row", "col"),
            P("row", "col"),
            P("col", "row"),
            P("row", "col"),
            P("row"),
            P(),
            P(),
        ),
        out_specs=(P("row", "col"), P("col", "row"), P("row", "col"), P("row"), P("col")),
        check_vma=False,
    )
```

```python
import functools

import jax
import jax.numpy as jnp
from jax import lax
from jax.experimental import pallas as pl
from jax.experimental.pallas import tpu as pltpu
from jax.sharding import PartitionSpec as P

TILE_T = 8
TILE_F = 128
MESH = pl.DeviceIdType.MESH


mix_one = 73856093
mix_two = 19349663
mix_three = 83492791
golden = -1640531535
mult_one = 2146121005
mult_two = -2073254261


def shift_down(value, count):
    return lax.shift_right_logical(value, jnp.full(value.shape, count, jnp.int32))


def keep_mask(tile_keys, stream_ids, first_tile, tile_count, per_chunk):
    salt = (
        stream_ids[0] * jnp.int32(mix_one)
        ^ stream_ids[1] * jnp.int32(mix_two)
        ^ stream_ids[2] * jnp.int32(mix_three)
    )
    token_tiles = tile_keys.shape[0]
    chunks = tile_count // per_chunk
    keys = lax.dynamic_slice_in_dim(tile_keys, first_tile, tile_count, 1) ^ salt
    keys = keys.reshape(token_tiles, chunks, per_chunk).transpose(1, 0, 2)
    shape = (chunks, token_tiles, TILE_T, per_chunk, TILE_F)
    offset = lax.broadcasted_iota(jnp.int32, shape, 2) * TILE_F + lax.broadcasted_iota(
        jnp.int32, shape, 4
    )
    value = keys[:, :, None, :, None] + offset * jnp.int32(golden)
    value = value ^ shift_down(value, 16)
    value = value * jnp.int32(mult_one)
    value = value ^ shift_down(value, 15)
    value = value * jnp.int32(mult_two)
    value = value ^ shift_down(value, 16)
    keep = (shift_down(value, 8) & jnp.int32(1023)) < jnp.int32(922)
    return keep.astype(jnp.bfloat16).reshape(chunks, token_tiles * TILE_T, per_chunk * TILE_F)


def exchange_kernel(
    n, lag, units, slots, rows,
    tokens, grads, w_in, w_out, bias, keep,
    act, dpre, acc, bias_out,
    own, from_left, from_right, to_right, to_left, in_ring, out_ring,
    in_sem, out_sem, right_send, right_recv, left_send, left_recv,
    bias_sum, bias_landed, bias_send, bias_recv,
):
    me = lax.axis_index("col")
    right, left = lax.rem(me + 1, n), lax.rem(me + n - 1, n)
    total_rows, width = own.shape[1], own.shape[2]
    model = in_ring.shape[1]
    chunks = units // 2
    far = jnp.maximum(me, n - 1 - me) * lag

    def fetch_in(c):
        slot = lax.rem(c, slots)
        cols = pl.ds(pl.multiple_of(c * width, width), width)
        return pltpu.make_async_copy(w_in.at[:, cols], in_ring.at[slot], in_sem.at[slot])

    def fetch_out(c):
        slot = lax.rem(c, 2)
        cols = pl.ds(pl.multiple_of(c * width, width), width)
        return pltpu.make_async_copy(w_out.at[cols, :], out_ring.at[slot], out_sem.at[slot])

    def send_right(q):
        return pltpu.make_async_remote_copy(
            src_ref=to_right.at[lax.rem(q, 2)], dst_ref=from_left.at[q],
            send_sem=right_send.at[lax.rem(q, 2)], recv_sem=right_recv.at[q],
            device_id={"col": right}, device_id_type=MESH,
        )

    def send_left(q):
        return pltpu.make_async_remote_copy(
            src_ref=to_left.at[lax.rem(q, 2)], dst_ref=from_right.at[q],
            send_sem=left_send.at[lax.rem(q, 2)], recv_sem=left_recv.at[q],
            device_id={"col": left}, device_id_type=MESH,
        )

    def own_unit(q):
        c = q // 2

        @pl.when(lax.rem(q, 2) == 0)
        def _():
            fetch_in(c).wait()

            @pl.when(c + 1 < chunks)
            def _():
                fetch_in(c + 1).start()
                fetch_out(c + 1).start()

            own[q] = jnp.dot(
                tokens[...], in_ring[lax.rem(c, slots)], preferred_element_type=jnp.float32
            )

        @pl.when(lax.rem(q, 2) == 1)
        def _():
            fetch_out(c).wait()
            own[q] = lax.dot_general(
                grads[...], out_ring[lax.rem(c, 2)], (((1,), (1,)), ((), ())),
                preferred_element_type=jnp.float32,
            )

    def pass_on(arrived, outgoing, copy, q, first, last):
        @pl.when(jnp.logical_not(first))
        def _():
            copy(q).wait_recv()

        @pl.when(jnp.logical_not(last))
        def _():
            @pl.when(q >= 2)
            def _():
                copy(q - 2).wait_send()

            @pl.when(first)
            def _():
                outgoing[lax.rem(q, 2)] = own[q].astype(outgoing.dtype)

            @pl.when(jnp.logical_not(first))
            def _():
                outgoing[lax.rem(q, 2)] = (
                    arrived[q].astype(jnp.float32) + own[q]
                ).astype(outgoing.dtype)

            copy(q).start()

    def finish(c):
        cols = pl.ds(pl.multiple_of(c * width, width), width)
        shift = bias[c]

        def whole(q, at):
            return (
                own[q, at, :]
                + from_left[q, at, :].astype(jnp.float32)
                + from_right[q, at, :].astype(jnp.float32)
            )

        def block(k, total):
            at = pl.ds(pl.multiple_of(k * rows, rows), rows)
            pre = whole(2 * c, at) + shift
            scaled = keep[c, at, :].astype(jnp.float32) * (1.0 / 0.9)
            cdf = 0.5 * (1.0 + lax.erf(pre * 0.7071067811865476))
            act[at, cols] = (pre * cdf * scaled).astype(act.dtype)
            slope = cdf + pre * jnp.exp(-0.5 * pre * pre) * 0.3989422804014327
            part = (whole(2 * c + 1, at) * scaled * slope).astype(dpre.dtype)
            dpre[at, cols] = part
            return total + jnp.sum(part.astype(jnp.float32), axis=0, keepdims=True)

        bias_sum[c] = lax.fori_loop(
            0, total_rows // rows, block, jnp.zeros((1, width), jnp.float32)
        )
        slot = lax.rem(c, slots)

        def into(j, carry):
            at = pl.ds(pl.multiple_of(j * width, width), width)
            acc[:, at] += lax.dot_general(
                dpre[:, cols], in_ring[slot, at, :], (((1,), (1,)), ((), ())),
                preferred_element_type=jnp.float32,
            )
            return carry

        lax.fori_loop(0, model // width, into, 0)

    fetch_in(0).start()
    fetch_out(0).start()
    barrier = pltpu.get_barrier_semaphore()

    for k in range(1, n):
        pl.semaphore_signal(
            barrier, inc=1, device_id={"col": lax.rem(me + k, n)}, device_id_type=MESH
        )

    def clear(buffer):
        def one(q, carry):
            buffer[q] = jnp.zeros(buffer.shape[1:], buffer.dtype)
            return carry

        lax.fori_loop(0, units, one, 0)

    @pl.when(me == 0)
    def _():
        clear(from_left)

    @pl.when(me == n - 1)
    def _():
        clear(from_right)

    acc[...] = jnp.zeros_like(acc)
    own_unit(0)

    pl.semaphore_wait(barrier, n - 1)

    def step(s, carry):
        right_unit = s - me * lag
        left_unit = s - (n - 1 - me) * lag
        done = s - far

        @pl.when((right_unit >= 0) & (right_unit < units))
        def _():
            pass_on(from_left, to_right, send_right, right_unit, me == 0, me == n - 1)

        @pl.when((left_unit >= 0) & (left_unit < units))
        def _():
            pass_on(from_right, to_left, send_left, left_unit, me == n - 1, me == 0)

        @pl.when(s + 1 < units)
        def _():
            own_unit(s + 1)

        @pl.when((done >= 0) & (done < units) & (lax.rem(done + 2 * n * lag, 2) == 1))
        def _():
            finish(done // 2)

        return carry

    lax.fori_loop(0, units + (n - 1) * lag, step, 0)

    for q in (units - 2, units - 1):
        @pl.when(me < n - 1)
        def _():
            send_right(q).wait_send()

        @pl.when(me > 0)
        def _():
            send_left(q).wait_send()

    def share_bias(k):
        return pltpu.make_async_remote_copy(
            src_ref=bias_sum, dst_ref=bias_landed,
            send_sem=bias_send.at[k], recv_sem=bias_recv,
            device_id={"col": lax.rem(me + k, n)}, device_id_type=MESH,
        )

    @pl.when(me == 0)
    def _():
        for k in range(1, n):
            share_bias(k).start()
        bias_out[...] = bias_sum[...]
        for k in range(1, n):
            share_bias(k).wait_send()

    @pl.when(me > 0)
    def _():
        share_bias(1).wait_recv()
        bias_out[...] = bias_landed[...]


def exchange(all_tokens, all_grads, w_in, w_out, bias, keep, n):
    total_rows, model = all_tokens.shape
    ff_local = w_in.shape[1]
    chunks, _, width = keep.shape
    units = 2 * chunks
    lag = 2
    slots = (n - 1) * lag // 2 + 3
    vmem = pl.BlockSpec(memory_space=pltpu.VMEM)
    anywhere = pl.BlockSpec(memory_space=pl.ANY)
    unit_buffer = pltpu.VMEM((units, total_rows, width), jnp.bfloat16)
    unit_sems = pltpu.SemaphoreType.DMA((units,))
    return pl.pallas_call(
        functools.partial(exchange_kernel, n, lag, units, slots, 32),
        out_shape=(
            jax.ShapeDtypeStruct((total_rows, ff_local), jnp.bfloat16),
            jax.ShapeDtypeStruct((total_rows, ff_local), jnp.bfloat16),
            jax.ShapeDtypeStruct((total_rows, model), jnp.float32),
            jax.ShapeDtypeStruct((chunks, 1, width), jnp.float32),
        ),
        in_specs=[vmem, vmem, anywhere, anywhere, vmem, vmem],
        out_specs=(vmem, vmem, vmem, vmem),
        scratch_shapes=[
            pltpu.VMEM((units, total_rows, width), jnp.float32),
            unit_buffer,
            unit_buffer,
            pltpu.VMEM((2, total_rows, width), jnp.bfloat16),
            pltpu.VMEM((2, total_rows, width), jnp.bfloat16),
            pltpu.VMEM((slots, model, width), jnp.bfloat16),
            pltpu.VMEM((2, width, model), jnp.bfloat16),
            pltpu.SemaphoreType.DMA((slots,)),
            pltpu.SemaphoreType.DMA((2,)),
            pltpu.SemaphoreType.DMA((2,)),
            unit_sems,
            pltpu.SemaphoreType.DMA((2,)),
            unit_sems,
            pltpu.VMEM((chunks, 1, width), jnp.float32),
            pltpu.VMEM((chunks, 1, width), jnp.float32),
            pltpu.SemaphoreType.DMA((n,)),
            pltpu.SemaphoreType.DMA,
        ],
        compiler_params=pltpu.CompilerParams(
            collective_id=0, has_side_effects=True, vmem_limit_bytes=63 * 1024 * 1024
        ),
        cost_estimate=pl.CostEstimate(
            flops=6 * total_rows * model * ff_local,
            bytes_accessed=4 * model * ff_local,
            transcendentals=2 * total_rows * ff_local,
        ),
    )(all_tokens, all_grads, w_in, w_out, bias, keep)


def gather_kernel(count, tokens, grads, all_tokens, all_grads,
                  here, far_send, far_recv, mate_send, mate_recv):
    me = lax.axis_index("row")
    mate = me + 1 - 2 * lax.rem(me, 2)
    half = count // 2
    pairs = ((tokens, all_tokens), (grads, all_grads))
    barrier = pltpu.get_barrier_semaphore()
    for k in range(1, half):
        pl.semaphore_signal(
            barrier, inc=1, device_id={"row": lax.rem(me + 2 * k, count)}, device_id_type=MESH
        )
    pl.semaphore_signal(barrier, inc=1, device_id={"row": mate}, device_id_type=MESH)
    keeps = [
        pltpu.make_async_copy(src, dst.at[me], here.at[a]) for a, (src, dst) in enumerate(pairs)
    ]
    for copy in keeps:
        copy.start()
    pl.semaphore_wait(barrier, half)

    def to_far(a, k):
        src, dst = pairs[a]
        return pltpu.make_async_remote_copy(
            src_ref=src, dst_ref=dst.at[me],
            send_sem=far_send.at[a, k], recv_sem=far_recv.at[a, k],
            device_id={"row": lax.rem(me + 2 * k, count)}, device_id_type=MESH,
        )

    def to_mate(a, k):
        src, dst = pairs[a]
        origin = lax.rem(me + count - 2 * k, count)
        return pltpu.make_async_remote_copy(
            src_ref=src if k == 0 else dst.at[origin], dst_ref=dst.at[origin],
            send_sem=mate_send.at[a, k], recv_sem=mate_recv.at[a, k],
            device_id={"row": mate}, device_id_type=MESH,
        )

    for a in range(2):
        for k in range(1, half):
            to_far(a, k).start()
    for a in range(2):
        to_mate(a, 0).start()
    for a in range(2):
        for k in range(1, half):
            to_far(a, k).wait_recv()
            to_mate(a, k).start()
    for a in range(2):
        for k in range(1, half):
            to_far(a, k).wait_send()
        for k in range(half):
            to_mate(a, k).wait()
        keeps[a].wait()


def gather_rows(tokens, grads):
    count = lax.axis_size("row")
    rows, model = tokens.shape
    anywhere = pl.BlockSpec(memory_space=pl.ANY)
    shape = jax.ShapeDtypeStruct((count, rows, model), tokens.dtype)
    sems = pltpu.SemaphoreType.DMA((2, count // 2))
    all_tokens, all_grads = pl.pallas_call(
        functools.partial(gather_kernel, count),
        out_shape=(shape, shape),
        in_specs=[anywhere, anywhere],
        out_specs=(anywhere, anywhere),
        scratch_shapes=[pltpu.SemaphoreType.DMA((2,)), sems, sems, sems, sems],
        compiler_params=pltpu.CompilerParams(collective_id=1, has_side_effects=True),
    )(tokens, grads)
    return (all_tokens.reshape(count * rows, model), all_grads.reshape(count * rows, model))


def weight_grad_kernel(left, right, out):
    columns = out.shape[1]
    step = 512 if columns % 512 == 0 else columns
    for start in range(0, columns, step):
        out[:, start:start + step] = lax.dot_general(
            left[...], right[:, start:start + step], (((0,), (0,)), ((), ())),
            preferred_element_type=jnp.float32,
        ).astype(out.dtype)


def weight_grad(left, right):
    tokens, rows = left.shape
    columns = right.shape[1]
    tile = 256
    return pl.pallas_call(
        weight_grad_kernel,
        out_shape=jax.ShapeDtypeStruct((rows, columns), jnp.bfloat16),
        grid=(rows // tile,),
        in_specs=[
            pl.BlockSpec((tokens, tile), lambda i: (0, i)),
            pl.BlockSpec((tokens, columns), lambda i: (0, 0)),
        ],
        out_specs=pl.BlockSpec((tile, columns), lambda i: (i, 0)),
        compiler_params=pltpu.CompilerParams(vmem_limit_bytes=32 * 1024 * 1024),
        cost_estimate=pl.CostEstimate(
            flops=2 * tokens * rows * columns,
            bytes_accessed=2 * (rows * columns + tokens * (rows + columns)),
            transcendentals=0,
        ),
    )(left, right)


def scatter_rows(terms):
    count = lax.axis_size("row")
    me = lax.axis_index("row")
    half = count // 2
    group, side = me // 2, lax.rem(me, 2)
    terms = terms.reshape(half, 2, terms.shape[0] // count, terms.shape[1])
    other = lax.dynamic_index_in_dim(terms, 1 - side, 1, keepdims=False).astype(jnp.bfloat16)
    other = lax.ppermute(other, "row", [(r, r + 1 - 2 * (r % 2)) for r in range(count)])
    mine = lax.dynamic_index_in_dim(terms, side, 1, keepdims=False) + other.astype(jnp.float32)
    total = lax.dynamic_index_in_dim(mine, group, 0, keepdims=False)
    for k in range(1, half):
        block = lax.dynamic_index_in_dim(mine, lax.rem(group + k, half), 0, keepdims=False)
        block = lax.ppermute(
            block.astype(jnp.bfloat16), "row", [(r, (r + 2 * k) % count) for r in range(count)]
        )
        total = total + block.astype(jnp.float32)
    return total.astype(jnp.bfloat16)


def local(tokens, out_grad, w_in, w_out, bias_in, stream_ids, tile_keys):
    col_count = lax.axis_size("col")
    row_index = lax.axis_index("row")
    ff_local = w_in.shape[1]
    width = 256
    chunks = ff_local // width
    all_tokens, all_grads = gather_rows(tokens, out_grad)
    tile_count = ff_local // TILE_F
    keep = keep_mask(tile_keys, stream_ids, row_index * tile_count, tile_count, width // TILE_F)
    act, dpre, token_terms, bias_sum = exchange(
        all_tokens, all_grads, w_in, w_out, bias_in.reshape(chunks, 1, width), keep, col_count
    )
    grad_tokens = scatter_rows(token_terms)
    grad_w_out = weight_grad(act, all_grads)
    grad_w_in = weight_grad(all_tokens, dpre)
    grad_bias_in = bias_sum.reshape(ff_local)
    grad_bias_out = jnp.sum(all_grads.astype(jnp.float32), axis=0)
    return (grad_tokens, grad_w_in, grad_w_out, grad_bias_in, grad_bias_out)


def solution(mesh):
    return jax.shard_map(
        local,
        mesh=mesh,
        in_specs=(
            P("row", "col"),
            P("row", "col"),
            P("col", "row"),
            P("row", "col"),
            P("row"),
            P(),
            P(),
        ),
        out_specs=(P("row", "col"), P("col", "row"), P("row", "col"), P("row"), P("col")),
        check_vma=False,
    )
```

```python
import functools

import jax
import jax.numpy as jnp
from jax import lax
from jax.experimental import pallas as pl
from jax.experimental.pallas import tpu as pltpu
from jax.sharding import PartitionSpec as P

TILE_T = 8
TILE_F = 128
MESH = pl.DeviceIdType.MESH


mix_one = 73856093
mix_two = 19349663
mix_three = 83492791
golden = -1640531535
mult_one = 2146121005
mult_two = -2073254261


def shift_down(value, count):
    return lax.shift_right_logical(value, jnp.full(value.shape, count, jnp.int32))


def salted_keys(tile_keys, stream_ids, first_tile, tile_count):
    salt = (
        stream_ids[0] * jnp.int32(mix_one)
        ^ stream_ids[1] * jnp.int32(mix_two)
        ^ stream_ids[2] * jnp.int32(mix_three)
    )
    return lax.dynamic_slice_in_dim(tile_keys, first_tile, tile_count, 1) ^ salt


def keep_tile(key, offset):
    value = key + offset
    value = value ^ shift_down(value, 16)
    value = value * jnp.int32(mult_one)
    value = value ^ shift_down(value, 15)
    value = value * jnp.int32(mult_two)
    value = value ^ shift_down(value, 16)
    kept = (shift_down(value, 8) & jnp.int32(1023)) < jnp.int32(922)
    return jnp.where(kept, 1.0, 0.0)


def write_keep(keys, keep):
    token_tiles, tile_count = keys.shape
    per_chunk = keep.shape[2] // TILE_F
    tile = (TILE_T, TILE_F)
    offset = (
        lax.broadcasted_iota(jnp.int32, tile, 0) * TILE_F + lax.broadcasted_iota(jnp.int32, tile, 1)
    ) * jnp.int32(golden)

    def pair(t, carry):
        at = pl.ds(pl.multiple_of(t * 2 * TILE_T, 2 * TILE_T), 2 * TILE_T)
        for j in range(tile_count):
            start = j % per_chunk * TILE_F
            both = [keep_tile(keys[2 * t + half, j], offset) for half in range(2)]
            keep[j // per_chunk, at, start:start + TILE_F] = jnp.concatenate(both, 0).astype(
                keep.dtype
            )
        return carry

    lax.fori_loop(0, token_tiles // 2, pair, 0)


def exchange_kernel(
    n, lag, units, slots, rows,
    tokens, grads, w_in, w_out, bias, keep,
    act, dpre, acc, bias_out,
    own, from_left, from_right, to_right, to_left, in_ring, out_ring,
    in_sem, out_sem, right_send, right_recv, left_send, left_recv,
    bias_sum, bias_landed, bias_send, bias_recv,
):
    me = lax.axis_index("col")
    right, left = lax.rem(me + 1, n), lax.rem(me + n - 1, n)
    total_rows, width = own.shape[1], own.shape[2]
    model = in_ring.shape[1]
    chunks = units // 2
    far = jnp.maximum(me, n - 1 - me) * lag

    def fetch_in(c):
        slot = lax.rem(c, slots)
        cols = pl.ds(pl.multiple_of(c * width, width), width)
        return pltpu.make_async_copy(w_in.at[:, cols], in_ring.at[slot], in_sem.at[slot])

    def fetch_out(c):
        slot = lax.rem(c, 2)
        cols = pl.ds(pl.multiple_of(c * width, width), width)
        return pltpu.make_async_copy(w_out.at[cols, :], out_ring.at[slot], out_sem.at[slot])

    def send_right(q):
        return pltpu.make_async_remote_copy(
            src_ref=to_right.at[lax.rem(q, 2)], dst_ref=from_left.at[q],
            send_sem=right_send.at[lax.rem(q, 2)], recv_sem=right_recv.at[q],
            device_id={"col": right}, device_id_type=MESH,
        )

    def send_left(q):
        return pltpu.make_async_remote_copy(
            src_ref=to_left.at[lax.rem(q, 2)], dst_ref=from_right.at[q],
            send_sem=left_send.at[lax.rem(q, 2)], recv_sem=left_recv.at[q],
            device_id={"col": left}, device_id_type=MESH,
        )

    def own_unit(q):
        c = q // 2

        @pl.when(lax.rem(q, 2) == 0)
        def _():
            fetch_in(c).wait()

            @pl.when(c + 1 < chunks)
            def _():
                fetch_in(c + 1).start()
                fetch_out(c + 1).start()

            own[q] = jnp.dot(
                tokens[...], in_ring[lax.rem(c, slots)], preferred_element_type=jnp.float32
            )

        @pl.when(lax.rem(q, 2) == 1)
        def _():
            fetch_out(c).wait()
            own[q] = lax.dot_general(
                grads[...], out_ring[lax.rem(c, 2)], (((1,), (1,)), ((), ())),
                preferred_element_type=jnp.float32,
            )

    def pass_on(arrived, outgoing, copy, q, first, last):
        @pl.when(jnp.logical_not(first))
        def _():
            copy(q).wait_recv()

        @pl.when(jnp.logical_not(last))
        def _():
            @pl.when(q >= 2)
            def _():
                copy(q - 2).wait_send()

            @pl.when(first)
            def _():
                outgoing[lax.rem(q, 2)] = own[q].astype(outgoing.dtype)

            @pl.when(jnp.logical_not(first))
            def _():
                outgoing[lax.rem(q, 2)] = (
                    arrived[q].astype(jnp.float32) + own[q]
                ).astype(outgoing.dtype)

            copy(q).start()

    def finish(c):
        cols = pl.ds(pl.multiple_of(c * width, width), width)
        shift = bias[c]

        def whole(q, at):
            return (
                own[q, at, :]
                + from_left[q, at, :].astype(jnp.float32)
                + from_right[q, at, :].astype(jnp.float32)
            )

        def block(k, total):
            at = pl.ds(pl.multiple_of(k * rows, rows), rows)
            pre = whole(2 * c, at) + shift
            scaled = keep[c, at, :].astype(jnp.float32) * (1.0 / 0.9)
            cdf = 0.5 * (1.0 + lax.erf(pre * 0.7071067811865476))
            act[at, cols] = (pre * cdf * scaled).astype(act.dtype)
            slope = cdf + pre * jnp.exp(-0.5 * pre * pre) * 0.3989422804014327
            part = (whole(2 * c + 1, at) * scaled * slope).astype(dpre.dtype)
            dpre[at, cols] = part
            return total + jnp.sum(part.astype(jnp.float32), axis=0, keepdims=True)

        bias_sum[c] = lax.fori_loop(
            0, total_rows // rows, block, jnp.zeros((1, width), jnp.float32)
        )
        slot = lax.rem(c, slots)

        def into(j, carry):
            at = pl.ds(pl.multiple_of(j * width, width), width)
            acc[:, at] += lax.dot_general(
                dpre[:, cols], in_ring[slot, at, :], (((1,), (1,)), ((), ())),
                preferred_element_type=jnp.float32,
            )
            return carry

        lax.fori_loop(0, model // width, into, 0)

    fetch_in(0).start()
    fetch_out(0).start()
    barrier = pltpu.get_barrier_semaphore()

    for k in range(1, n):
        pl.semaphore_signal(
            barrier, inc=1, device_id={"col": lax.rem(me + k, n)}, device_id_type=MESH
        )

    def clear(buffer):
        def one(q, carry):
            buffer[q] = jnp.zeros(buffer.shape[1:], buffer.dtype)
            return carry

        lax.fori_loop(0, units, one, 0)

    @pl.when(me == 0)
    def _():
        clear(from_left)

    @pl.when(me == n - 1)
    def _():
        clear(from_right)

    acc[...] = jnp.zeros_like(acc)
    own_unit(0)

    pl.semaphore_wait(barrier, n - 1)

    def step(s, carry):
        right_unit = s - me * lag
        left_unit = s - (n - 1 - me) * lag
        done = s - far

        @pl.when((right_unit >= 0) & (right_unit < units))
        def _():
            pass_on(from_left, to_right, send_right, right_unit, me == 0, me == n - 1)

        @pl.when((left_unit >= 0) & (left_unit < units))
        def _():
            pass_on(from_right, to_left, send_left, left_unit, me == n - 1, me == 0)

        @pl.when(s + 1 < units)
        def _():
            own_unit(s + 1)

        @pl.when((done >= 0) & (done < units) & (lax.rem(done + 2 * n * lag, 2) == 1))
        def _():
            finish(done // 2)

        return carry

    lax.fori_loop(0, units + (n - 1) * lag, step, 0)

    for q in (units - 2, units - 1):
        @pl.when(me < n - 1)
        def _():
            send_right(q).wait_send()

        @pl.when(me > 0)
        def _():
            send_left(q).wait_send()

    def share_bias(k):
        return pltpu.make_async_remote_copy(
            src_ref=bias_sum, dst_ref=bias_landed,
            send_sem=bias_send.at[k], recv_sem=bias_recv,
            device_id={"col": lax.rem(me + k, n)}, device_id_type=MESH,
        )

    @pl.when(me == 0)
    def _():
        for k in range(1, n):
            share_bias(k).start()
        bias_out[...] = bias_sum[...]
        for k in range(1, n):
            share_bias(k).wait_send()

    @pl.when(me > 0)
    def _():
        share_bias(1).wait_recv()
        bias_out[...] = bias_landed[...]


def exchange(all_tokens, all_grads, w_in, w_out, bias, keep, n):
    total_rows, model = all_tokens.shape
    ff_local = w_in.shape[1]
    chunks, _, width = keep.shape
    units = 2 * chunks
    lag = 2
    slots = (n - 1) * lag // 2 + 3
    vmem = pl.BlockSpec(memory_space=pltpu.VMEM)
    anywhere = pl.BlockSpec(memory_space=pl.ANY)
    unit_buffer = pltpu.VMEM((units, total_rows, width), jnp.bfloat16)
    unit_sems = pltpu.SemaphoreType.DMA((units,))
    return pl.pallas_call(
        functools.partial(exchange_kernel, n, lag, units, slots, 32),
        out_shape=(
            jax.ShapeDtypeStruct((total_rows, ff_local), jnp.bfloat16),
            jax.ShapeDtypeStruct((total_rows, ff_local), jnp.bfloat16),
            jax.ShapeDtypeStruct((total_rows, model), jnp.float32),
            jax.ShapeDtypeStruct((chunks, 1, width), jnp.float32),
        ),
        in_specs=[vmem, vmem, anywhere, anywhere, vmem, vmem],
        out_specs=(vmem, vmem, vmem, vmem),
        scratch_shapes=[
            pltpu.VMEM((units, total_rows, width), jnp.float32),
            unit_buffer,
            unit_buffer,
            pltpu.VMEM((2, total_rows, width), jnp.bfloat16),
            pltpu.VMEM((2, total_rows, width), jnp.bfloat16),
            pltpu.VMEM((slots, model, width), jnp.bfloat16),
            pltpu.VMEM((2, width, model), jnp.bfloat16),
            pltpu.SemaphoreType.DMA((slots,)),
            pltpu.SemaphoreType.DMA((2,)),
            pltpu.SemaphoreType.DMA((2,)),
            unit_sems,
            pltpu.SemaphoreType.DMA((2,)),
            unit_sems,
            pltpu.VMEM((chunks, 1, width), jnp.float32),
            pltpu.VMEM((chunks, 1, width), jnp.float32),
            pltpu.SemaphoreType.DMA((n,)),
            pltpu.SemaphoreType.DMA,
        ],
        compiler_params=pltpu.CompilerParams(
            collective_id=0, has_side_effects=True, vmem_limit_bytes=63 * 1024 * 1024
        ),
        cost_estimate=pl.CostEstimate(
            flops=6 * total_rows * model * ff_local,
            bytes_accessed=4 * model * ff_local,
            transcendentals=2 * total_rows * ff_local,
        ),
    )(all_tokens, all_grads, w_in, w_out, bias, keep)


def gather_kernel(count, tokens, grads, keys, all_tokens, all_grads, keep,
                  here, far_send, far_recv, mate_send, mate_recv):
    me = lax.axis_index("row")
    mate = me + 1 - 2 * lax.rem(me, 2)
    half = count // 2
    pairs = ((tokens, all_tokens), (grads, all_grads))
    barrier = pltpu.get_barrier_semaphore()
    for k in range(1, half):
        pl.semaphore_signal(
            barrier, inc=1, device_id={"row": lax.rem(me + 2 * k, count)}, device_id_type=MESH
        )
    pl.semaphore_signal(barrier, inc=1, device_id={"row": mate}, device_id_type=MESH)
    keeps = [
        pltpu.make_async_copy(src, dst.at[me], here.at[a]) for a, (src, dst) in enumerate(pairs)
    ]
    for copy in keeps:
        copy.start()
    pl.semaphore_wait(barrier, half)

    def to_far(a, k):
        src, dst = pairs[a]
        return pltpu.make_async_remote_copy(
            src_ref=src, dst_ref=dst.at[me],
            send_sem=far_send.at[a, k], recv_sem=far_recv.at[a, k],
            device_id={"row": lax.rem(me + 2 * k, count)}, device_id_type=MESH,
        )

    def to_mate(a, k):
        src, dst = pairs[a]
        origin = lax.rem(me + count - 2 * k, count)
        return pltpu.make_async_remote_copy(
            src_ref=src if k == 0 else dst.at[origin], dst_ref=dst.at[origin],
            send_sem=mate_send.at[a, k], recv_sem=mate_recv.at[a, k],
            device_id={"row": mate}, device_id_type=MESH,
        )

    for a in range(2):
        for k in range(1, half):
            to_far(a, k).start()
    for a in range(2):
        to_mate(a, 0).start()
    write_keep(keys, keep)
    for a in range(2):
        for k in range(1, half):
            to_far(a, k).wait_recv()
            to_mate(a, k).start()
    for a in range(2):
        for k in range(1, half):
            to_far(a, k).wait_send()
        for k in range(half):
            to_mate(a, k).wait()
        keeps[a].wait()


def gather_rows(tokens, grads, keys, width):
    count = lax.axis_size("row")
    rows, model = tokens.shape
    anywhere = pl.BlockSpec(memory_space=pl.ANY)
    shape = jax.ShapeDtypeStruct((count, rows, model), tokens.dtype)
    sems = pltpu.SemaphoreType.DMA((2, count // 2))
    kept = (keys.shape[1] * TILE_F // width, count * rows, width)
    all_tokens, all_grads, keep = pl.pallas_call(
        functools.partial(gather_kernel, count),
        out_shape=(shape, shape, jax.ShapeDtypeStruct(kept, jnp.bfloat16)),
        in_specs=[anywhere, anywhere, pl.BlockSpec(memory_space=pltpu.SMEM)],
        out_specs=(anywhere, anywhere, pl.BlockSpec(memory_space=pltpu.VMEM)),
        scratch_shapes=[pltpu.SemaphoreType.DMA((2,)), sems, sems, sems, sems],
        compiler_params=pltpu.CompilerParams(
            collective_id=1, has_side_effects=True, vmem_limit_bytes=32 * 1024 * 1024
        ),
    )(tokens, grads, keys)
    whole = (count * rows, model)
    return (all_tokens.reshape(whole), all_grads.reshape(whole), keep)


def weight_grad_kernel(left, right, out):
    columns = out.shape[1]
    step = 512 if columns % 512 == 0 else columns
    for start in range(0, columns, step):
        out[:, start:start + step] = lax.dot_general(
            left[...], right[:, start:start + step], (((0,), (0,)), ((), ())),
            preferred_element_type=jnp.float32,
        ).astype(out.dtype)


def weight_grad(left, right):
    tokens, rows = left.shape
    columns = right.shape[1]
    tile = 256
    return pl.pallas_call(
        weight_grad_kernel,
        out_shape=jax.ShapeDtypeStruct((rows, columns), jnp.bfloat16),
        grid=(rows // tile,),
        in_specs=[
            pl.BlockSpec((tokens, tile), lambda i: (0, i)),
            pl.BlockSpec((tokens, columns), lambda i: (0, 0)),
        ],
        out_specs=pl.BlockSpec((tile, columns), lambda i: (i, 0)),
        compiler_params=pltpu.CompilerParams(vmem_limit_bytes=32 * 1024 * 1024),
        cost_estimate=pl.CostEstimate(
            flops=2 * tokens * rows * columns,
            bytes_accessed=2 * (rows * columns + tokens * (rows + columns)),
            transcendentals=0,
        ),
    )(left, right)


def scatter_rows(terms):
    count = lax.axis_size("row")
    me = lax.axis_index("row")
    half = count // 2
    group, side = me // 2, lax.rem(me, 2)
    terms = terms.reshape(half, 2, terms.shape[0] // count, terms.shape[1])
    other = lax.dynamic_index_in_dim(terms, 1 - side, 1, keepdims=False).astype(jnp.bfloat16)
    other = lax.ppermute(other, "row", [(r, r + 1 - 2 * (r % 2)) for r in range(count)])
    mine = lax.dynamic_index_in_dim(terms, side, 1, keepdims=False) + other.astype(jnp.float32)
    total = lax.dynamic_index_in_dim(mine, group, 0, keepdims=False)
    for k in range(1, half):
        block = lax.dynamic_index_in_dim(mine, lax.rem(group + k, half), 0, keepdims=False)
        block = lax.ppermute(
            block.astype(jnp.bfloat16), "row", [(r, (r + 2 * k) % count) for r in range(count)]
        )
        total = total + block.astype(jnp.float32)
    return total.astype(jnp.bfloat16)


def local(tokens, out_grad, w_in, w_out, bias_in, stream_ids, tile_keys):
    col_count = lax.axis_size("col")
    row_index = lax.axis_index("row")
    ff_local = w_in.shape[1]
    width = 256
    chunks = ff_local // width
    tile_count = ff_local // TILE_F
    keys = salted_keys(tile_keys, stream_ids, row_index * tile_count, tile_count)
    all_tokens, all_grads, keep = gather_rows(tokens, out_grad, keys, width)
    act, dpre, token_terms, bias_sum = exchange(
        all_tokens, all_grads, w_in, w_out, bias_in.reshape(chunks, 1, width), keep, col_count
    )
    grad_tokens = scatter_rows(token_terms)
    grad_w_out = weight_grad(act, all_grads)
    grad_w_in = weight_grad(all_tokens, dpre)
    grad_bias_in = bias_sum.reshape(ff_local)
    grad_bias_out = jnp.sum(all_grads.astype(jnp.float32), axis=0)
    return (grad_tokens, grad_w_in, grad_w_out, grad_bias_in, grad_bias_out)


def solution(mesh):
    return jax.shard_map(
        local,
        mesh=mesh,
        in_specs=(
            P("row", "col"),
            P("row", "col"),
            P("col", "row"),
            P("row", "col"),
            P("row"),
            P(),
            P(),
        ),
        out_specs=(P("row", "col"), P("col", "row"), P("row", "col"), P("row"), P("col")),
        check_vma=False,
    )
```
